32 devices in a mesh: space: 4 (over y, x), tm: 8 (over z, core).
Axes of the slice: x: 2, y: 2, z: 4, core: 2. Of those that a mesh axis runs over, the one named last changes fastest.
Arguments:
- initial_guess: float32 [4, 64, 32, 4, 128], P(None, 'tm', 'space'), may hold values from -6 to 6
- forcing: float32 [4, 64, 32, 4, 128], P(None, 'tm', 'space'), may hold values from -6 to 6
- visc_table: float32 [8], replicated, may hold values from 0.05 to 0.5
- visc_class: int32 [32, 4, 128], P('space'), may hold values from 0 to 7
- inverse_bank: bfloat16 [4, 32, 32], replicated, may hold values from -0.125 to 0.125
- patch_kind: int32 [16, 2, 64], P('space'), may hold values from 0 to 3
Outputs:
- smoothed: float32 [4, 64, 32, 4, 128], P(None, 'tm', 'space')
- coarse: float32 [4, 2, 16384], P(None, None, ('space', 'tm'))
The draws below stay inside these ranges and needn't reach their ends.
All inputs are finite; a program needn't handle non-finite values.
Results may differ from the reference program's by a relative error of at most 0.00096.
Values sent between devices are 32-bit elements; how exact they have to be, the bound alone decides.
No kernel may reach another device: no remote copies, remote signals or barrier semaphores. Data moves between devices by JAX's collectives and lax.ppermute only.
A program may use at most 64 MiB of HBM per device.

```python
import math
import jax
import jax.numpy as jnp
from jax import lax

NY = 4
NZ = 128
TS = 8
SWEEPS = 2
LEVELS = 5
KCLASS = 8
KINDS = 4
NX = 32
NT = 64


def set_ends(result, stream_key, least, high):
    longest = result.shape.index(max(result.shape))
    spots = []
    for shift in (0, 1):
        where = [jax.random.randint(jax.random.fold_in(stream_key, axis), (), 0, length) for axis, length in enumerate(result.shape)]
        where[longest] = (where[longest] + shift) % result.shape[longest]
        spots.append(tuple(where))
    return result.at[spots[0]].set(least).at[spots[1]].set(high)


def block_levels(rng, shape, shards, smallest, largest):
    def one(axis_at, shards_of):
        draws = jax.random.uniform(jax.random.fold_in(jax.random.fold_in(rng, 6), axis_at), (shards_of,), jnp.float32, smallest / len(shards), largest / len(shards))
        return jnp.repeat(jnp.exp(draws), shape[axis_at] // shards_of).reshape((-1,) + (1,) * (len(shape) - axis_at - 1))

    factor_of = one(*shards[0])
    for cut in shards[1:]:
        factor_of = factor_of * one(*cut)
    return factor_of


def normal_values(stream_key, extent, scale, most, shards=(), kind=jnp.bfloat16):
    values = scale * jax.random.normal(stream_key, extent, jnp.float32)
    if shards:
        values = values * block_levels(stream_key, extent, shards, -0.22, 0.18)
    return jnp.clip(values, -most, most).astype(kind)


def setup_inputs(seed: int = 0) -> dict:
    key_list = jax.random.split(jax.random.key(seed), 7)
    initial_guess = normal_values(key_list[0], (4, NT, NX, NY, NZ), 1.0, 6.0, ((1, 8), (2, 4)), jnp.float32)
    forcing = normal_values(key_list[1], (4, NT, NX, NY, NZ), 1.0, 6.0, ((1, 8), (2, 4)), jnp.float32)
    visc_table = jnp.clip(jnp.exp(jax.random.uniform(key_list[2], (KCLASS,), jnp.float32, math.log(0.05), math.log(0.5))), 0.05, 0.5)
    visc_class = set_ends(jax.random.randint(key_list[3], (NX, NY, NZ), 0, KCLASS), jax.random.fold_in(key_list[3], 1), 0, KCLASS - 1).astype(jnp.int32)
    inverse_bank = normal_values(key_list[4], (KINDS, 32, 32), 2048 ** -0.5, 0.125)
    patch_kind = set_ends(jax.random.randint(key_list[5], (NX // 2, NY // 2, NZ // 2), 0, KINDS), jax.random.fold_in(key_list[5], 1), 0, KINDS - 1).astype(jnp.int32)
    return dict(initial_guess=initial_guess, forcing=forcing, visc_table=visc_table, visc_class=visc_class, inverse_bank=inverse_bank, patch_kind=patch_kind)


damping = 0.8
mass_weight = 1.0
stabilize = 0.1


def neighbour(array, offset):
    size_x = array.shape[-3] - 2
    size_y = array.shape[-2] - 2
    size_z = array.shape[-1] - 2
    return array[..., 1 + offset[0]:1 + offset[0] + size_x, 1 + offset[1]:1 + offset[1] + size_y, 1 + offset[2]:1 + offset[2] + size_z]


def operate(padded, earlier, visc_pad):
    extended = jnp.pad(padded, ((0, 0), (0, 0), (0, 0), (1, 1), (1, 1)))
    viscous = jnp.pad(visc_pad, ((0, 0), (1, 1), (1, 1)))
    centre = (0, 0, 0)
    centre_visc = neighbour(viscous, centre)
    velocity = neighbour(extended[:3], centre)
    pressure = neighbour(extended[3], centre)
    units = ((1, 0, 0), (0, 1, 0), (0, 0, 1))
    diffusion = jnp.zeros_like(velocity)
    pressure_sum = jnp.zeros_like(pressure)
    gradient = []
    divergence = jnp.zeros_like(pressure)
    for number in range(3):
        unit = units[number]
        minus = (-unit[0], -unit[1], -unit[2])
        for offset in (unit, minus):
            kappa = 0.5 * (centre_visc + neighbour(viscous, offset))
            diffusion = diffusion + kappa * (velocity - neighbour(extended[:3], offset))
            pressure_sum = pressure_sum + neighbour(extended[3], offset)
        gradient.append(0.5 * (neighbour(extended[3], unit) - neighbour(extended[3], minus)))
        divergence = divergence + 0.5 * (neighbour(extended[number], unit) - neighbour(extended[number], minus))
    previous = jnp.concatenate([earlier[:, None], velocity[:, :-1]], axis=1)
    momentum = mass_weight * (velocity - previous) + diffusion + jnp.stack(gradient)
    continuity = stabilize * (6.0 * pressure - pressure_sum) - divergence
    return jnp.concatenate([momentum, continuity[None]], axis=0)


def lookup(classes, table):
    labels = jnp.arange(table.shape[0], dtype=jnp.int32).reshape(-1, 1, 1, 1)
    return jnp.sum(jnp.where(classes[None] == labels, table.reshape(-1, 1, 1, 1), 0.0), axis=0)


def vanka_patches(resid, inverse_bank, patch_kind):
    kinds_count = inverse_bank.shape[0]
    comps, steps, size_x, size_y, size_z = resid.shape
    grouped = resid.reshape(comps, steps, size_x // 2, 2, size_y // 2, 2, size_z // 2, 2)
    grouped = grouped.transpose(0, 3, 5, 7, 1, 2, 4, 6).reshape(8 * comps, -1).astype(jnp.bfloat16)
    products = jnp.dot(inverse_bank.reshape(-1, 8 * comps), grouped, preferred_element_type=jnp.float32)
    products = products.reshape(kinds_count, 8 * comps, steps, size_x // 2, size_y // 2, size_z // 2)
    labels = jnp.arange(kinds_count, dtype=jnp.int32).reshape(-1, 1, 1, 1, 1, 1)
    chosen = jnp.sum(jnp.where(patch_kind[None, None, None] == labels, products, 0.0), axis=0)
    placed = (damping * chosen).reshape(comps, 2, 2, 2, steps, size_x // 2, size_y // 2, size_z // 2)
    return placed.transpose(0, 4, 5, 1, 6, 2, 7, 3).reshape(comps, steps, size_x, size_y, size_z)


def coarsen(level_now, before_step):
    even_steps = level_now[:, 0::2]
    odd_steps = level_now[:, 1::2]
    shifted = jnp.concatenate([before_step[:, None], odd_steps[:, :-1]], axis=1)
    return 0.25 * shifted + 0.5 * even_steps + 0.25 * odd_steps


def reference(initial_guess, forcing, visc_table, visc_class, inverse_bank, patch_kind):
    viscosity = lookup(visc_class, visc_table)
    visc_pad = jnp.pad(viscosity, ((1, 1), (0, 0), (0, 0)))

    def blockwise(iterate, finish):
        def one_block(index):
            start = index * TS
            current = lax.dynamic_slice_in_dim(iterate, start, TS, 1)
            earlier = lax.dynamic_slice_in_dim(iterate, jnp.maximum(start - 1, 0), 1, 1)[:3, 0]
            earlier = jnp.where(index > 0, earlier, jnp.zeros_like(earlier))
            padded = jnp.pad(current, ((0, 0), (0, 0), (1, 1), (0, 0), (0, 0)))
            resid = lax.dynamic_slice_in_dim(forcing, start, TS, 1) - operate(padded, earlier, visc_pad)
            if finish:
                return resid
            return current + vanka_patches(resid, inverse_bank, patch_kind)

        blocks = lax.map(one_block, jnp.arange(NT // TS, dtype=jnp.int32))
        return jnp.moveaxis(blocks, 0, 1).reshape(4, NT, NX, NY, NZ)

    iterate = initial_guess
    for sweep_index in range(SWEEPS):
        iterate = blockwise(iterate, False)
    final = blockwise(iterate, True).reshape(4, NT, NX * NY * NZ)
    coarse = final
    for level_index in range(LEVELS):
        coarse = coarsen(coarse, jnp.zeros_like(coarse[:, 0]))
    return iterate, coarse
```

```python
import functools

import jax
import jax.numpy as jnp
from jax import lax
from jax.experimental import pallas as pl
from jax.experimental.pallas import tpu as pltpu
from jax.sharding import PartitionSpec as P

SWEEPS = 2
LEVELS = 5
FACTOR = 2**LEVELS

damping = 0.8
stabilize = 0.1

F32 = jnp.float32
BF16 = jnp.bfloat16

TILE = 8
PLANE = 4


def hat(step, k):
    far = step - FACTOR * k
    far = jnp.where(far < 0, -far, far)
    return jnp.where(far < FACTOR, FACTOR - far, 0).astype(F32) * (1.0 / FACTOR**2)


def lane_ids(shape):
    return lax.broadcasted_iota(jnp.int32, shape, 1)


def row_ids(shape):
    return lax.broadcasted_iota(jnp.int32, shape, 0)


def rolled(tile, by):
    return pltpu.roll(tile, by % tile.shape[1], 1)


def edge_masks():
    shape = (TILE, 128)
    row = row_ids(shape) % PLANE
    lane = lane_ids(shape)
    one = lambda keep: jnp.where(keep, 1.0, 0.0).astype(F32)
    return one(row < PLANE - 1), one(row > 0), one(lane < 127), one(lane > 0)


def coefficients(visc_pad, base, masks):
    v = visc_pad[base : base + 8]
    around = (
        visc_pad[base + 4 : base + 12],
        visc_pad[base - 4 : base + 4],
        masks[0] * visc_pad[base + 1 : base + 9],
        masks[1] * visc_pad[base - 1 : base + 7],
        masks[2] * rolled(v, -1),
        masks[3] * rolled(v, 1),
    )
    kappas = [0.5 * (v + other) for other in around]
    diagonal = sum(kappas[1:], kappas[0])
    kept = kappas[:2] + [mask * kappa for mask, kappa in zip(masks, kappas[2:])]
    return diagonal, kept


def neighbours(at, base, masks=None):
    centre = at(base)
    y_up, y_down = at(base + 1), at(base - 1)
    z_up, z_down = rolled(centre, -1), rolled(centre, 1)
    if masks is not None:
        y_up, y_down, z_up, z_down = (
            masks[0] * y_up,
            masks[1] * y_down,
            masks[2] * z_up,
            masks[3] * z_down,
        )
    return centre, (at(base + 4), at(base - 4), y_up, y_down, z_up, z_down)


def space_operator(ats, base, coefs, masks):
    diagonal, kappas = coefs
    pressure, beside = neighbours(ats[3], base, masks)
    total = sum(beside[1:], beside[0])
    out = []
    divergence = None
    for c in range(3):
        centre, near = neighbours(ats[c], base)
        spread = sum((k * f for k, f in zip(kappas[1:], near[1:])), kappas[0] * near[0])
        slope = 0.5 * (beside[2 * c] - beside[2 * c + 1])
        out.append(diagonal * centre - spread + slope)
        up, down = near[2 * c], near[2 * c + 1]
        if c > 0:
            up, down = masks[2 * c - 2] * up, masks[2 * c - 1] * down
        part = up - down
        divergence = part if divergence is None else divergence + part
    out.append(stabilize * (6.0 * pressure - total) - 0.5 * divergence)
    return out


def residual(ats, before, forcing, base, coefs, masks):
    applied = space_operator(ats, base, coefs, masks)
    out = []
    for c in range(3):
        out.append(forcing[c] - (ats[c](base) - before[c]) - applied[c])
    out.append(forcing[3] - applied[3])
    return out


def kind_masks(kind_tile, kinds):
    out = []
    for k in range(kinds):
        mask = jnp.where(kind_tile == float(k), 1.0, 0.0).astype(F32)
        out.append(jnp.concatenate([mask] * 8, axis=0).astype(BF16))
    return out


def put_operand(x_ref, at, tiles, masks):
    same = jnp.concatenate(tiles, axis=0)
    even = lane_ids(same.shape) % 2 == 0
    other = jnp.where(even, rolled(same, -1), rolled(same, 1))
    both = jnp.concatenate([same, other], axis=0).astype(BF16)
    for k, mask in enumerate(masks):
        x_ref[64 * k : 64 * k + 64, 128 * at : 128 * at + 128] = both * mask


def patch_product(w_ref, x_ref, count):
    return jnp.dot(w_ref[...], x_ref[:, : 128 * count], preferred_element_type=F32)


def taken(product, at):
    first = product[:32, 128 * at : 128 * at + 128]
    second = product[32:, 128 * at : 128 * at + 128]
    chosen = jnp.where(lane_ids(first.shape) % 2 == 0, first, second)
    return [damping * chosen[8 * c : 8 * c + 8] for c in range(4)]


def side_slots():
    odd = lax.axis_index("space") % 2
    return odd ^ 1, odd


def tiles_at(ref, n):
    return [lambda row, c=c: ref[c, n, row : row + 8] for c in range(4)]


def tables_kernel(table_ref, class_ref, bank_ref, kind_ref, visc_ref, kinds_ref, w_ref, rows_ref):
    planes = class_ref.shape[0]
    for x in range(planes):
        classes = class_ref[x]
        found = jnp.zeros(classes.shape, F32)
        for k in range(table_ref.shape[0]):
            found = jnp.where(classes == k, table_ref[k], found)
        visc_ref[PLANE * x : PLANE * x + PLANE] = found

    groups = kind_ref.shape[0]
    for g in range(groups):
        rows_ref[2 * g : 2 * g + 2] = kind_ref[g].astype(F32)
    rows = PLANE * planes
    shape = (rows, 2 * groups)
    r = row_ids(shape)
    spread_rows = jnp.where(lane_ids(shape) == r // 8 * 2 + r % 4 // 2, 1.0, 0.0).astype(BF16)
    shape = (64, 128)
    spread_lanes = jnp.where(row_ids(shape) == lane_ids(shape) // 2, 1.0, 0.0).astype(BF16)
    wide = jnp.dot(rows_ref[...].astype(BF16), spread_lanes, preferred_element_type=F32)
    kinds_ref[...] = jnp.dot(spread_rows, wide.astype(BF16), preferred_element_type=F32)

    shape = (32, 64)
    same_y = row_ids(shape) // 2 % 2 == lane_ids(shape) // 2 % 2
    for p in range(2):
        shape = (32, 32)
        r = row_ids(shape)
        left = jnp.where(lane_ids(shape) == r // 4 * 4 + r % 2 * 2 + p, 1.0, 0.0).astype(BF16)
        shape = (32, 64)
        q = lane_ids(shape)
        side = (p + q // 32) % 2
        at = q % 32
        right = jnp.where(row_ids(shape) == at // 4 * 4 + at % 2 * 2 + side, 1.0, 0.0).astype(BF16)
        for k in range(bank_ref.shape[0]):
            half = jnp.dot(bank_ref[k], right, preferred_element_type=F32).astype(BF16)
            full = jnp.dot(left, half, preferred_element_type=F32)
            w_ref[32 * p : 32 * p + 32, 64 * k : 64 * k + 64] = jnp.where(same_y, full, 0.0).astype(BF16)


def tail_kernel(guess_ref, forcing_ref, out_ref):
    out_ref[:, 0] = guess_ref[:, 1]
    out_ref[0:3, 1] = forcing_ref[0:3, 0] + guess_ref[0:3, 0]
    out_ref[3, 1] = forcing_ref[3, 0]


def first_message_kernel(low_ref, high_ref, t_low_ref, t_high_ref, visc_ref, kinds_ref, a_ref, b_ref):
    steps = low_ref.shape[1]
    rows = visc_ref.shape[0]
    left, _ = side_slots()

    def fill(to_left, to_right):
        for ref, edge, t_edge, first, row in (
            (to_left, low_ref, t_low_ref, 0, 0),
            (to_right, high_ref, t_high_ref, 4, rows - 4),
        ):
            for c in range(4):
                at = c * (steps + 1) * 4
                ref[at : at + 4] = t_edge[c, 0, first : first + 4]
                for n in range(steps):
                    ref[at + 4 + 4 * n : at + 8 + 4 * n] = edge[c, n, first : first + 4]
            at = 16 * (steps + 1)
            ref[at : at + 4] = visc_ref[row : row + 4]
            ref[at + 4 : at + 8] = kinds_ref[row : row + 4]

    @pl.when(left == 0)
    def _():
        fill(a_ref, b_ref)

    @pl.when(left == 1)
    def _():
        fill(b_ref, a_ref)


def first_sweep(g, offset, ats, guess, guess_ref, forcing_ref, t_ref, coefs, masks, kinds_ref, w_ref, x_ref, put):
    steps = forcing_ref.shape[1]
    base = offset + TILE * g
    own = slice(TILE * g, TILE * g + TILE)
    chosen = kind_masks(kinds_ref[own], w_ref.shape[1] // 64)
    for n in range(-1, steps):
        if n < 0:
            applied = space_operator(ats(n), base, coefs, masks)
            tiles = [t_ref[c, 1, own] - (t_ref[c, 0, own] if c < 3 else 0.0) - applied[c] for c in range(4)]
        else:
            force = [forcing_ref[c, n, own] for c in range(4)]
            before = [t_ref[c, 0, own] if n == 0 else guess_ref[c, n - 1, own] for c in range(3)]
            tiles = residual(ats(n), before, force, base, coefs, masks)
        put_operand(x_ref, n + 1, tiles, chosen)
    product = patch_product(w_ref, x_ref, steps + 1)
    for n in range(-1, steps):
        change = taken(product, n + 1)
        put(n, own, [guess(c, n, own) + change[c] for c in range(4)])


def first_inner_kernel(guess_ref, forcing_ref, t_ref, visc_ref, kinds_ref, w_ref, inner_ref, x_ref):
    rows = guess_ref.shape[2]
    masks = edge_masks()

    def ats(n):
        return tiles_at(t_ref, 0) if n < 0 else tiles_at(guess_ref, n)

    def guess(c, n, own):
        return t_ref[c, 0, own] if n < 0 else guess_ref[c, n, own]

    def put(n, own, values):
        for c in range(4):
            inner_ref[c, n + 1, own.start - TILE : own.stop - TILE] = values[c]

    for g in range(1, rows // TILE - 1):
        coefs = coefficients(visc_ref, TILE * g, masks)
        first_sweep(
            g, 0, ats, guess, guess_ref, forcing_ref, t_ref, coefs, masks, kinds_ref, w_ref, x_ref, put
        )


def by_side(which, work):
    left, _ = side_slots()

    @pl.when(left == which)
    def _():
        work(0)

    @pl.when(left != which)
    def _():
        work(1)


def local_rows(side, rows):
    if side == 0:
        return slice(8, 20), slice(0, 12)
    return slice(4, 16), slice(rows - 12, rows)


def first_side_kernel(
    guess_ref,
    forcing_ref,
    t_ref,
    inner_ref,
    in_ref,
    visc_ref,
    kinds_ref,
    w_ref,
    *refs,
    which,
    coarse,
):
    if which:
        straight_ref, it_ref, out_ref, visc_loc, passed_ref, u_ref, v_ref, x_ref = refs
        passed_ref[...] = straight_ref[...]
    else:
        it_ref, out_ref, visc_loc, u_ref, v_ref, x_ref = refs
    steps, rows = guess_ref.shape[1], guess_ref.shape[2]
    start = lax.axis_index("tm") * steps
    masks = edge_masks()
    weights = [[hat(start + n, k) for n in range(steps)] for k in range(coarse)]
    count = 16 * steps

    def work(side):
        g = 0 if side == 0 else rows // TILE - 1
        own = slice(TILE * g, TILE * g + TILE)
        there, here = local_rows(side, rows)
        halo = slice(4, 8) if side == 0 else slice(16, 20)
        u_ref[:, 0, there] = t_ref[:, 0, here]
        u_ref[:, 1 : 1 + steps, there] = guess_ref[:, :, here]
        for c in range(4):
            for n in range(steps + 1):
                at = (c * (steps + 1) + n) * 4
                u_ref[c, n, halo] = in_ref[at : at + 4]
        at = 16 * (steps + 1)
        visc_loc[there] = visc_ref[here]
        visc_loc[halo] = in_ref[at : at + 4]
        coefs = coefficients(visc_loc, 8, masks)

        def ats(n):
            return tiles_at(u_ref, n + 1)

        def guess(c, n, own):
            return u_ref[c, n + 1, 8:16]

        def put(n, own, values):
            for c in range(4):
                it_ref[c, n + 1] = values[c]

        first_sweep(
            g, 8 - TILE * g, ats, guess, guess_ref, forcing_ref, t_ref, coefs, masks, kinds_ref, w_ref, x_ref, put
        )

        v_ref[:, :, halo] = jnp.zeros((4, steps, 4, 128), F32)
        v_ref[:, :, 8:16] = it_ref[:, 1:]
        if side == 0:
            v_ref[:, :, 16:20] = inner_ref[:, 1:, 0:4]
        else:
            v_ref[:, :, 4:8] = inner_ref[:, 1:, rows - 2 * TILE - 4 : rows - 2 * TILE]
        edge, inner = (0, 4) if side == 0 else (4, 0)
        sums = [[None] * coarse for _ in range(4)]
        for n in range(steps):
            force = [forcing_ref[c, n, own] for c in range(4)]
            before = [it_ref[c, n] for c in range(3)]
            tiles = residual(tiles_at(v_ref, n), before, force, 8, coefs, masks)
            for c in range(4):
                at = (c * steps + n) * 4
                out_ref[at : at + 4] = v_ref[c, n, 8 + edge : 12 + edge]
                out_ref[count + at : count + at + 4] = tiles[c][edge : edge + 4]
                rounded = tiles[c].astype(BF16).astype(F32)
                for k in range(coarse):
                    part = weights[k][n] * rounded
                    sums[c][k] = part if n == 0 else sums[c][k] + part
        for c in range(4):
            for k in range(coarse):
                at = 2 * count + (c * coarse + k) * 4
                out_ref[at : at + 4] = sums[c][k][inner : inner + 4]

    by_side(which, work)


class Restriction:
    def __init__(self, weights, forcing_ref, smooth_ref, shift):
        self.weights, self.forcing_ref, self.smooth_ref, self.shift = weights, forcing_ref, smooth_ref, shift
        self.held = [[None] * len(weights) for _ in range(4)]
        self.rest = [[None] * len(weights) for _ in range(4)]

    def put(self, n, own, values):
        for c in range(4):
            self.smooth_ref[c, n, own.start + self.shift : own.stop + self.shift] = values[c]
            force = self.forcing_ref[c, n, own]
            for k, weight in enumerate(self.weights):
                one, two = weight[n] * values[c], weight[n] * force
                if c < 3:
                    two = two - (weight[n] - weight[n + 1]) * values[c]
                self.held[c][k] = one if n == 0 else self.held[c][k] + one
                self.rest[c][k] = two if n == 0 else self.rest[c][k] + two


def block_weights(steps, coarse):
    start = lax.axis_index("tm") * steps
    return [[hat(start + n, k) for n in range(steps + 1)] for k in range(coarse)]


def second_sweep(g, offset, u_ref, shift, it_ref, it_own, forcing_ref, coefs, masks, kinds_ref, w_ref, x_ref, put):
    steps = forcing_ref.shape[1]
    base = offset + TILE * g
    own = slice(TILE * g, TILE * g + TILE)
    chosen = kind_masks(kinds_ref[own], w_ref.shape[1] // 64)
    for n in range(steps):
        force = [forcing_ref[c, n, own] for c in range(4)]
        before = [it_ref[c, n, it_own] for c in range(3)]
        put_operand(x_ref, n, residual(tiles_at(u_ref, n + shift), before, force, base, coefs, masks), chosen)
    product = patch_product(w_ref, x_ref, steps)
    for n in range(steps):
        change = taken(product, n)
        put(n, own, [it_ref[c, n + 1, it_own] + change[c] for c in range(4)])


def second_inner_kernel(
    a_ref, b_ref, inner_ref, forcing_ref, visc_ref, kinds_ref, w_ref, smooth_ref, sums_ref, it_ref, x_ref
):
    steps, rows = forcing_ref.shape[1], forcing_ref.shape[2]
    coarse = sums_ref.shape[3]
    masks = edge_masks()
    weights = block_weights(steps, coarse)
    it_ref[:, :, TILE : rows - TILE] = inner_ref[...]

    def work(side):
        low, high = (a_ref, b_ref) if side == 0 else (b_ref, a_ref)
        it_ref[:, :, 0:TILE] = low[...]
        it_ref[:, :, rows - TILE : rows] = high[...]

    by_side(0, work)
    for g in range(1, rows // TILE - 1):
        sums = Restriction(weights, forcing_ref, smooth_ref, -TILE)
        coefs = coefficients(visc_ref, TILE * g, masks)
        own = slice(TILE * g, TILE * g + TILE)
        second_sweep(
            g, 0, it_ref, 1, it_ref, own, forcing_ref, coefs, masks, kinds_ref, w_ref, x_ref, sums.put
        )
        for c in range(4):
            for k in range(coarse):
                sums_ref[g - 1, 0, c, k] = sums.held[c][k]
                sums_ref[g - 1, 1, c, k] = sums.rest[c][k]


def second_side_kernel(
    it_ref,
    inner_ref,
    forcing_ref,
    first_ref,
    in_ref,
    visc_loc,
    kinds_ref,
    w_ref,
    after_ref,
    smooth_ref,
    sums_ref,
    halo_ref,
    v_ref,
    x_ref,
    *,
    which,
):
    steps, rows = forcing_ref.shape[1], forcing_ref.shape[2]
    coarse = sums_ref.shape[2]
    kinds = w_ref.shape[1] // 64
    space = lax.axis_index("space")
    count = 16 * steps
    static = 16 * (steps + 1)
    masks = edge_masks()
    weights = block_weights(steps, coarse)

    def work(side):
        g = 0 if side == 0 else rows // TILE - 1
        if side == 0:
            inside, outer, edge, sign = 8, 4, 4, 1.0
            exists = space > 0
            v_ref[:, :, 16:20] = inner_ref[:, 1:, 0:4]
        else:
            inside, outer, edge, sign = 12, 16, 0, -1.0
            exists = space < lax.axis_size("space") - 1
            v_ref[:, :, 4:8] = inner_ref[:, 1:, rows - 2 * TILE - 4 : rows - 2 * TILE]
        v_ref[:, :, 8:16] = it_ref[:, 1:]
        for c in range(4):
            for n in range(steps):
                at = (c * steps + n) * 4
                v_ref[c, n, outer : outer + 4] = in_ref[at : at + 4]

        kappa = 0.5 * (visc_loc[inside : inside + 4] + visc_loc[outer : outer + 4])
        sums = [[None] * coarse for _ in range(4)]
        plain = [[None] * coarse for _ in range(4)]
        for n in range(steps):
            mine = [v_ref[c, n, inside : inside + 4] for c in range(4)]
            add = [kappa * mine[c] for c in range(3)]
            add[0] = add[0] - (0.5 * sign) * mine[3]
            add.append(stabilize * mine[3] + (0.5 * sign) * mine[0])
            for c in range(4):
                at = count + (c * steps + n) * 4
                rounded = (in_ref[at : at + 4] + add[c]).astype(BF16).astype(F32)
                value = v_ref[c, n, outer : outer + 4]
                for k in range(coarse):
                    one, two = weights[k][n] * rounded, weights[k][n] * value
                    sums[c][k] = one if n == 0 else sums[c][k] + one
                    plain[c][k] = two if n == 0 else plain[c][k] + two
        beside = first_ref[static + 4 : static + 8]
        chosen = kind_masks(jnp.concatenate([beside] * 2, axis=0), kinds)
        for k in range(coarse):
            tiles = []
            for c in range(4):
                at = 2 * count + (c * coarse + k) * 4
                far = in_ref[at : at + 4]
                pair = [far, sums[c][k]] if side == 0 else [sums[c][k], far]
                tiles.append(jnp.concatenate(pair, axis=0))
            high = [tile.astype(BF16).astype(F32) for tile in tiles]
            put_operand(x_ref, 2 * k, high, chosen)
            put_operand(x_ref, 2 * k + 1, [t - h for t, h in zip(tiles, high)], chosen)
        product = patch_product(w_ref, x_ref, 2 * coarse)
        exists = jnp.where(exists, 1.0, 0.0).astype(F32)
        for k in range(coarse):
            one, two = taken(product, 2 * k), taken(product, 2 * k + 1)
            for c in range(4):
                change = (one[c] + two[c])[edge : edge + 4]
                halo_ref[c, k] = exists * (plain[c][k] + change)

        totals = Restriction(weights, forcing_ref, smooth_ref, -TILE * g)
        coefs = coefficients(visc_loc, 8, masks)
        second_sweep(
            g, 8 - TILE * g, v_ref, 0, it_ref, slice(0, 8), forcing_ref, coefs, masks, kinds_ref, w_ref, x_ref, totals.put
        )
        for c in range(4):
            for k in range(coarse):
                sums_ref[0, c, k] = totals.held[c][k]
                sums_ref[1, c, k] = totals.rest[c][k]

    by_side(which, work)


def parts_kernel(
    a_sums_ref,
    b_sums_ref,
    a_halo_ref,
    b_halo_ref,
    a_visc_ref,
    b_visc_ref,
    inner_sums_ref,
    visc_ref,
    keep_ref,
    give_ref,
    s_ref,
    rest_ref,
    visc_pad,
    part_ref,
):
    size_t, _, coarse, share, _ = part_ref.shape
    rows = visc_ref.shape[0]
    groups = rows // TILE
    end = 8 + rows
    visc_pad[8:end] = visc_ref[...]
    s_ref[:, :, 16 : end - 8] = jnp.concatenate([inner_sums_ref[g, 0] for g in range(groups - 2)], axis=2)
    rest_ref[:, :, 8 : rows - 8] = jnp.concatenate([inner_sums_ref[g, 1] for g in range(groups - 2)], axis=2)

    def work(side):
        a = (a_sums_ref, a_halo_ref, a_visc_ref)
        b = (b_sums_ref, b_halo_ref, b_visc_ref)
        low, high = (a, b) if side == 0 else (b, a)
        s_ref[:, :, 8:16] = low[0][0]
        s_ref[:, :, end - 8 : end] = high[0][0]
        rest_ref[:, :, 0:8] = low[0][1]
        rest_ref[:, :, rows - 8 : rows] = high[0][1]
        s_ref[:, :, 4:8] = low[1][...]
        s_ref[:, :, end : end + 4] = high[1][...]
        visc_pad[4:8] = low[2][4:8]
        visc_pad[end : end + 4] = high[2][16:20]

    by_side(0, work)
    masks = edge_masks()
    for g in range(groups):
        base = 8 + TILE * g
        coefs = coefficients(visc_pad, base, masks)
        for k in range(coarse):
            applied = space_operator(tiles_at(s_ref, k), base, coefs, masks)
            for c in range(4):
                value = rest_ref[c, k, TILE * g : TILE * g + TILE] - applied[c]
                for row in range(0, TILE, share):
                    part_ref[(TILE * g + row) // share, c, k] = value[row : row + share]
    core = lax.axis_index("tm") % 2
    for i in range(size_t // 2):
        keep_ref[i] = part_ref[2 * i + core]
        give_ref[i] = part_ref[2 * i + (1 - core)]


def join_kernel(a_ref, b_ref, inner_ref, smooth_ref):
    rows = smooth_ref.shape[2]
    smooth_ref[:, :, TILE : rows - TILE] = inner_ref[...]

    def work(side):
        low, high = (a_ref, b_ref) if side == 0 else (b_ref, a_ref)
        smooth_ref[:, :, 0:TILE] = low[...]
        smooth_ref[:, :, rows - TILE : rows] = high[...]

    by_side(0, work)


def pair_kernel(keep_ref, given_ref, *refs, order):
    out_refs, sum_ref = refs[:-1], refs[-1]
    chip = lax.axis_index("tm") // 2
    sum_ref[...] = keep_ref[...] + given_ref[...]
    for d, ref in zip(order, out_refs):
        ref[...] = sum_ref[chip ^ d]


def total_kernel(*refs):
    out_ref = refs[-1]
    total = refs[0][...]
    for ref in refs[1:-1]:
        total = total + ref[...]
    for row in range(total.shape[2]):
        out_ref[:, :, 128 * row : 128 * row + 128] = total[:, :, row]


def whole_spec():
    return pl.BlockSpec(memory_space=pltpu.VMEM)


def call(kernel, outs, ins, scratch=(), specs=None, flops=10**6, limit=24, **options):
    size = sum(a.size * a.dtype.itemsize for a in ins)
    size += sum(o.size * o.dtype.itemsize for o in outs)
    return pl.pallas_call(
        kernel,
        out_shape=outs,
        in_specs=specs or [whole_spec()] * len(ins),
        out_specs=[whole_spec()] * len(outs),
        scratch_shapes=list(scratch),
        compiler_params=pltpu.CompilerParams(vmem_limit_bytes=int(limit * 2**20)),
        cost_estimate=pl.CostEstimate(flops=flops, bytes_accessed=size, transcendentals=0),
        **options,
    )(*ins)


def swapped(messages):
    size = lax.axis_size("space")
    out = []
    for number, message in enumerate(messages):
        pairs = [(i, i + 1) for i in range(number, size - 1, 2)]
        out.append(lax.ppermute(message, "space", pairs + [(j, i) for i, j in pairs]))
    return out


def shape_of(*dims, kind=F32):
    return jax.ShapeDtypeStruct(dims, kind)


def per_device(initial_guess, forcing, visc_table, visc_class, inverse_bank, patch_kind):
    comps, steps, planes, ny, nz = initial_guess.shape
    rows = planes * ny
    guess = initial_guess.reshape(comps, steps, rows, nz)
    force = forcing.reshape(comps, steps, rows, nz)
    kinds = inverse_bank.shape[0]
    size_t = lax.axis_size("tm")
    coarse = steps * size_t // FACTOR
    half = size_t // 2
    share = rows // size_t

    (tail,) = call(
        tail_kernel,
        [shape_of(comps, 2, rows, nz)],
        [guess, force],
        specs=[
            pl.BlockSpec((comps, 2, rows, nz), lambda i: (0, steps // 2 - 1, 0, 0)),
            pl.BlockSpec((comps, 1, rows, nz), lambda i: (0, steps - 1, 0, 0)),
        ],
        limit=53.5,
        grid=(1,),
    )
    tail = lax.ppermute(tail, "tm", [(i, i + 1) for i in range(size_t - 1)])

    visc, kind_rows, weights = call(
        tables_kernel,
        [shape_of(rows, nz), shape_of(rows, nz), shape_of(64, 64 * kinds, kind=BF16)],
        [visc_table, visc_class, inverse_bank, patch_kind],
        [pltpu.VMEM((rows // 4, nz // 2), F32)],
        [pl.BlockSpec(memory_space=pltpu.SMEM)] + [whole_spec()] * 3,
    )

    last = rows // 8 - 1
    edge = (comps, steps, 8, nz)
    t_edge = (comps, 1, 8, nz)
    length = comps * (steps + 1) * 4 + 8
    first = call(
        first_message_kernel,
        [shape_of(length, nz)] * 2,
        [guess, guess, tail, tail, visc, kind_rows],
        specs=[
            pl.BlockSpec(edge, lambda i: (0, 0, 0, 0)),
            pl.BlockSpec(edge, lambda i: (0, 0, last, 0)),
            pl.BlockSpec(t_edge, lambda i: (0, 0, 0, 0)),
            pl.BlockSpec(t_edge, lambda i: (0, 0, last, 0)),
            whole_spec(),
            whole_spec(),
        ],
        grid=(1,),
    )
    first_in = swapped(first)

    field = shape_of(comps, steps, rows, nz)
    operand = pltpu.VMEM((64 * kinds, (steps + 1) * nz), BF16)
    (inner,) = call(
        first_inner_kernel,
        [shape_of(comps, steps + 1, rows - 2 * TILE, nz)],
        [guess, force, tail, visc, kind_rows, weights],
        [operand],
        flops=10**7,
    )
    length_2 = 8 * comps * steps + 4 * comps * coarse
    done = []
    message = shape_of(length_2, nz)
    for which in range(2):
        done.append(
            call(
                functools.partial(first_side_kernel, which=which, coarse=coarse),
                [shape_of(comps, steps + 1, TILE, nz), message, shape_of(24, nz)] + [message] * which,
                [guess, force, tail, inner, first_in[which], visc, kind_rows, weights]
                + [made[1] for made in done],
                [
                    pltpu.VMEM((comps, steps + 1, 24, nz), F32),
                    pltpu.VMEM((comps, steps, 24, nz), F32),
                    operand,
                ],
                flops=5 * 10**6,
            )
        )
    (straight, _, straight_visc), (diagonal, diagonal_message, diagonal_visc, straight_message) = done
    iterate, visc_loc = (straight, diagonal), (straight_visc, diagonal_visc)
    second = (straight_message, diagonal_message)
    second_in = swapped(second)

    inner_smooth, inner_sums = call(
        second_inner_kernel,
        [shape_of(comps, steps, rows - 2 * TILE, nz), shape_of(rows // TILE - 2, 2, comps, coarse, TILE, nz)],
        [*iterate, inner, force, visc, kind_rows, weights],
        [pltpu.VMEM((comps, steps + 1, rows, nz), F32), operand],
        flops=10**7,
    )
    done = []
    for which in range(2):
        done.append(
            call(
                functools.partial(second_side_kernel, which=which),
                [
                    shape_of(comps, steps, TILE, nz),
                    shape_of(2, comps, coarse, TILE, nz),
                    shape_of(comps, coarse, 4, nz),
                ],
                [iterate[which], inner, force, first_in[which], second_in[which]]
                + [visc_loc[which], kind_rows, weights, done[0][2] if which else visc],
                [
                    pltpu.VMEM((comps, steps, 24, nz), F32),
                    pltpu.VMEM((64 * kinds, max(steps, 2 * coarse) * nz), BF16),
                ],
                flops=5 * 10**6,
            )
        )
    smooth, sums, halo = zip(*done)
    piece = (comps, coarse, share, nz)
    keep, give = call(
        parts_kernel,
        [shape_of(half, *piece)] * 2,
        [*sums, *halo, *visc_loc, inner_sums, visc],
        [
            pltpu.VMEM((comps, coarse, rows + 16, nz), F32),
            pltpu.VMEM((comps, coarse, rows, nz), F32),
            pltpu.VMEM((rows + 16, nz), F32),
            pltpu.VMEM((size_t, *piece), F32),
        ],
    )
    given = lax.ppermute(give, "tm", [(i, i ^ 1) for i in range(size_t)])
    (smoothed,) = call(join_kernel, [field], [*smooth, inner_smooth])
    far_first = list(range(half - 1, 0, -1))
    far_first[:2] = far_first[1::-1]
    *others, own = call(
        functools.partial(pair_kernel, order=far_first + [0]),
        [shape_of(*piece)] * half,
        [keep, given],
        [pltpu.VMEM((half, *piece), F32)],
    )
    arrived = [
        lax.ppermute(other, "tm", [(i, i ^ (2 * d)) for i in range(size_t)])
        for d, other in zip(far_first, others)
    ]
    (result,) = call(total_kernel, [shape_of(comps, coarse, share * nz)], [*arrived, own])
    return (smoothed.reshape(initial_guess.shape), result)


def solution(mesh):
    return jax.shard_map(
        per_device,
        mesh=mesh,
        in_specs=(
            P(None, "tm", "space", None, None),
            P(None, "tm", "space", None, None),
            P(),
            P("space", None, None),
            P(),
            P("space", None, None),
        ),
        out_specs=(P(None, "tm", "space", None, None), P(None, None, ("space", "tm"))),
        check_vma=False,
    )
```

```python
import functools

import jax
import jax.numpy as jnp
from jax import lax
from jax.experimental import pallas as pl
from jax.experimental.pallas import tpu as pltpu
from jax.sharding import PartitionSpec as P

SWEEPS = 2
LEVELS = 5
FACTOR = 2**LEVELS

damping = 0.8
stabilize = 0.1

F32 = jnp.float32
BF16 = jnp.bfloat16

TILE = 8
PLANE = 4


def hat(step, k):
    far = step - FACTOR * k
    far = jnp.where(far < 0, -far, far)
    return jnp.where(far < FACTOR, FACTOR - far, 0).astype(F32) * (1.0 / FACTOR**2)


def lane_ids(shape):
    return lax.broadcasted_iota(jnp.int32, shape, 1)


def row_ids(shape):
    return lax.broadcasted_iota(jnp.int32, shape, 0)


def rolled(tile, by):
    return pltpu.roll(tile, by % tile.shape[1], 1)


def edge_masks():
    shape = (TILE, 128)
    row = row_ids(shape) % PLANE
    lane = lane_ids(shape)
    one = lambda keep: jnp.where(keep, 1.0, 0.0).astype(F32)
    return one(row < PLANE - 1), one(row > 0), one(lane < 127), one(lane > 0)


def coefficients(visc_pad, base, masks):
    v = visc_pad[base : base + 8]
    around = (
        visc_pad[base + 4 : base + 12],
        visc_pad[base - 4 : base + 4],
        masks[0] * visc_pad[base + 1 : base + 9],
        masks[1] * visc_pad[base - 1 : base + 7],
        masks[2] * rolled(v, -1),
        masks[3] * rolled(v, 1),
    )
    kappas = [0.5 * (v + other) for other in around]
    diagonal = sum(kappas[1:], kappas[0])
    kept = kappas[:2] + [mask * kappa for mask, kappa in zip(masks, kappas[2:])]
    return diagonal, kept


def neighbours(at, base, masks=None):
    centre = at(base)
    y_up, y_down = at(base + 1), at(base - 1)
    z_up, z_down = rolled(centre, -1), rolled(centre, 1)
    if masks is not None:
        y_up, y_down, z_up, z_down = (
            masks[0] * y_up,
            masks[1] * y_down,
            masks[2] * z_up,
            masks[3] * z_down,
        )
    return centre, (at(base + 4), at(base - 4), y_up, y_down, z_up, z_down)


def space_operator(ats, base, coefs, masks):
    diagonal, kappas = coefs
    pressure, beside = neighbours(ats[3], base, masks)
    total = sum(beside[1:], beside[0])
    out = []
    divergence = None
    for c in range(3):
        centre, near = neighbours(ats[c], base)
        spread = sum((k * f for k, f in zip(kappas[1:], near[1:])), kappas[0] * near[0])
        slope = 0.5 * (beside[2 * c] - beside[2 * c + 1])
        out.append(diagonal * centre - spread + slope)
        up, down = near[2 * c], near[2 * c + 1]
        if c > 0:
            up, down = masks[2 * c - 2] * up, masks[2 * c - 1] * down
        part = up - down
        divergence = part if divergence is None else divergence + part
    out.append(stabilize * (6.0 * pressure - total) - 0.5 * divergence)
    return out


def residual(ats, before, forcing, base, coefs, masks):
    applied = space_operator(ats, base, coefs, masks)
    out = []
    for c in range(3):
        out.append(forcing[c] - (ats[c](base) - before[c]) - applied[c])
    out.append(forcing[3] - applied[3])
    return out


def kind_masks(kind_tile, kinds):
    out = []
    for k in range(kinds):
        mask = jnp.where(kind_tile == float(k), 1.0, 0.0).astype(F32)
        out.append(jnp.concatenate([mask] * 8, axis=0).astype(BF16))
    return out


def put_operand(x_ref, at, tiles, masks):
    same = jnp.concatenate(tiles, axis=0)
    even = lane_ids(same.shape) % 2 == 0
    other = jnp.where(even, rolled(same, -1), rolled(same, 1))
    both = jnp.concatenate([same, other], axis=0).astype(BF16)
    for k, mask in enumerate(masks):
        x_ref[64 * k : 64 * k + 64, 128 * at : 128 * at + 128] = both * mask


def patch_product(w_ref, x_ref, count):
    return jnp.dot(w_ref[...], x_ref[:, : 128 * count], preferred_element_type=F32)


def taken(product, at):
    first = product[:32, 128 * at : 128 * at + 128]
    second = product[32:, 128 * at : 128 * at + 128]
    chosen = jnp.where(lane_ids(first.shape) % 2 == 0, first, second)
    return [damping * chosen[8 * c : 8 * c + 8] for c in range(4)]


def side_slots():
    odd = lax.axis_index("space") % 2
    return odd ^ 1, odd


def tiles_at(ref, n):
    return [lambda row, c=c: ref[c, n, row : row + 8] for c in range(4)]


def tables_kernel(table_ref, class_ref, bank_ref, kind_ref, visc_ref, kinds_ref, w_ref, rows_ref):
    planes = class_ref.shape[0]
    for x in range(planes):
        classes = class_ref[x]
        found = jnp.zeros(classes.shape, F32)
        for k in range(table_ref.shape[0]):
            found = jnp.where(classes == k, table_ref[k], found)
        visc_ref[PLANE * x : PLANE * x + PLANE] = found

    groups = kind_ref.shape[0]
    for g in range(groups):
        rows_ref[2 * g : 2 * g + 2] = kind_ref[g].astype(F32)
    rows = PLANE * planes
    shape = (rows, 2 * groups)
    r = row_ids(shape)
    spread_rows = jnp.where(lane_ids(shape) == r // 8 * 2 + r % 4 // 2, 1.0, 0.0).astype(BF16)
    shape = (64, 128)
    spread_lanes = jnp.where(row_ids(shape) == lane_ids(shape) // 2, 1.0, 0.0).astype(BF16)
    wide = jnp.dot(rows_ref[...].astype(BF16), spread_lanes, preferred_element_type=F32)
    kinds_ref[...] = jnp.dot(spread_rows, wide.astype(BF16), preferred_element_type=F32)

    shape = (32, 64)
    same_y = row_ids(shape) // 2 % 2 == lane_ids(shape) // 2 % 2
    for p in range(2):
        shape = (32, 32)
        r = row_ids(shape)
        left = jnp.where(lane_ids(shape) == r // 4 * 4 + r % 2 * 2 + p, 1.0, 0.0).astype(BF16)
        shape = (32, 64)
        q = lane_ids(shape)
        side = (p + q // 32) % 2
        at = q % 32
        right = jnp.where(row_ids(shape) == at // 4 * 4 + at % 2 * 2 + side, 1.0, 0.0).astype(BF16)
        for k in range(bank_ref.shape[0]):
            half = jnp.dot(bank_ref[k], right, preferred_element_type=F32).astype(BF16)
            full = jnp.dot(left, half, preferred_element_type=F32)
            w_ref[32 * p : 32 * p + 32, 64 * k : 64 * k + 64] = jnp.where(same_y, full, 0.0).astype(BF16)


def tail_kernel(guess_ref, forcing_ref, out_ref):
    out_ref[:, 0] = guess_ref[:, 1]
    out_ref[0:3, 1] = forcing_ref[0:3, 0] + guess_ref[0:3, 0]
    out_ref[3, 1] = forcing_ref[3, 0]


def first_message_kernel(low_ref, high_ref, t_low_ref, t_high_ref, visc_ref, kinds_ref, a_ref, b_ref):
    steps = low_ref.shape[1]
    rows = visc_ref.shape[0]
    left, _ = side_slots()

    def fill(to_left, to_right):
        for ref, edge, t_edge, first, row in (
            (to_left, low_ref, t_low_ref, 0, 0),
            (to_right, high_ref, t_high_ref, 4, rows - 4),
        ):
            for c in range(4):
                at = c * (steps + 1) * 4
                ref[at : at + 4] = t_edge[c, 0, first : first + 4]
                for n in range(steps):
                    ref[at + 4 + 4 * n : at + 8 + 4 * n] = edge[c, n, first : first + 4]
            at = 16 * (steps + 1)
            ref[at : at + 4] = visc_ref[row : row + 4]
            ref[at + 4 : at + 8] = kinds_ref[row : row + 4]

    @pl.when(left == 0)
    def _():
        fill(a_ref, b_ref)

    @pl.when(left == 1)
    def _():
        fill(b_ref, a_ref)


def first_sweep(g, offset, ats, guess, guess_ref, forcing_ref, t_ref, coefs, masks, kinds_ref, w_ref, x_ref, put):
    steps = forcing_ref.shape[1]
    base = offset + TILE * g
    own = slice(TILE * g, TILE * g + TILE)
    chosen = kind_masks(kinds_ref[own], w_ref.shape[1] // 64)
    for n in range(-1, steps):
        if n < 0:
            applied = space_operator(ats(n), base, coefs, masks)
            tiles = [t_ref[c, 1, own] - (t_ref[c, 0, own] if c < 3 else 0.0) - applied[c] for c in range(4)]
        else:
            force = [forcing_ref[c, n, own] for c in range(4)]
            before = [t_ref[c, 0, own] if n == 0 else guess_ref[c, n - 1, own] for c in range(3)]
            tiles = residual(ats(n), before, force, base, coefs, masks)
        put_operand(x_ref, n + 1, tiles, chosen)
    product = patch_product(w_ref, x_ref, steps + 1)
    for n in range(-1, steps):
        change = taken(product, n + 1)
        put(n, own, [guess(c, n, own) + change[c] for c in range(4)])


def first_inner_kernel(guess_ref, forcing_ref, t_ref, visc_ref, kinds_ref, w_ref, inner_ref, x_ref):
    rows = guess_ref.shape[2]
    masks = edge_masks()

    def ats(n):
        return tiles_at(t_ref, 0) if n < 0 else tiles_at(guess_ref, n)

    def guess(c, n, own):
        return t_ref[c, 0, own] if n < 0 else guess_ref[c, n, own]

    def put(n, own, values):
        for c in range(4):
            inner_ref[c, n + 1, own.start - TILE : own.stop - TILE] = values[c]

    for g in range(1, rows // TILE - 1):
        coefs = coefficients(visc_ref, TILE * g, masks)
        first_sweep(
            g, 0, ats, guess, guess_ref, forcing_ref, t_ref, coefs, masks, kinds_ref, w_ref, x_ref, put
        )


def by_side(which, work):
    left, _ = side_slots()

    @pl.when(left == which)
    def _():
        work(0)

    @pl.when(left != which)
    def _():
        work(1)


def local_rows(side, rows):
    if side == 0:
        return slice(8, 20), slice(0, 12)
    return slice(4, 16), slice(rows - 12, rows)


def first_side_kernel(
    guess_ref,
    forcing_ref,
    t_ref,
    inner_ref,
    in_ref,
    visc_ref,
    kinds_ref,
    w_ref,
    *refs,
    which,
    coarse,
):
    if which:
        _, it_ref, out_ref, visc_loc, u_ref, v_ref, x_ref = refs
    else:
        it_ref, out_ref, visc_loc, u_ref, x_ref = refs
    steps, rows = guess_ref.shape[1], guess_ref.shape[2]
    start = lax.axis_index("tm") * steps
    masks = edge_masks()
    weights = [[hat(start + n, k) for n in range(steps)] for k in range(coarse)]
    count = 16 * steps

    def work(side):
        g = 0 if side == 0 else rows // TILE - 1
        own = slice(TILE * g, TILE * g + TILE)
        there, here = local_rows(side, rows)
        halo = slice(4, 8) if side == 0 else slice(16, 20)
        u_ref[:, 0, there] = t_ref[:, 0, here]
        u_ref[:, 1 : 1 + steps, there] = guess_ref[:, :, here]
        for c in range(4):
            for n in range(steps + 1):
                at = (c * (steps + 1) + n) * 4
                u_ref[c, n, halo] = in_ref[at : at + 4]
        at = 16 * (steps + 1)
        visc_loc[there] = visc_ref[here]
        visc_loc[halo] = in_ref[at : at + 4]
        coefs = coefficients(visc_loc, 8, masks)

        def ats(n):
            return tiles_at(u_ref, n + 1)

        def guess(c, n, own):
            return u_ref[c, n + 1, 8:16]

        def put(n, own, values):
            for c in range(4):
                it_ref[c, n + 1] = values[c]

        first_sweep(
            g, 8 - TILE * g, ats, guess, guess_ref, forcing_ref, t_ref, coefs, masks, kinds_ref, w_ref, x_ref, put
        )

        edge, inner = (0, 4) if side == 0 else (4, 0)
        for c in range(4):
            for n in range(steps):
                at = (c * steps + n) * 4
                out_ref[at : at + 4] = it_ref[c, n + 1, edge : edge + 4]
        if not which:
            return

        v_ref[:, :, halo] = jnp.zeros((4, steps, 4, 128), F32)
        v_ref[:, :, 8:16] = it_ref[:, 1:]
        if side == 0:
            v_ref[:, :, 16:20] = inner_ref[:, 1:, 0:4]
        else:
            v_ref[:, :, 4:8] = inner_ref[:, 1:, rows - 2 * TILE - 4 : rows - 2 * TILE]
        sums = [[None] * coarse for _ in range(4)]
        for n in range(steps):
            force = [forcing_ref[c, n, own] for c in range(4)]
            before = [it_ref[c, n] for c in range(3)]
            tiles = residual(tiles_at(v_ref, n), before, force, 8, coefs, masks)
            for c in range(4):
                at = (c * steps + n) * 4
                out_ref[count + at : count + at + 4] = tiles[c][edge : edge + 4]
                rounded = tiles[c].astype(BF16).astype(F32)
                for k in range(coarse):
                    part = weights[k][n] * rounded
                    sums[c][k] = part if n == 0 else sums[c][k] + part
        for c in range(4):
            for k in range(coarse):
                at = 2 * count + (c * coarse + k) * 4
                out_ref[at : at + 4] = sums[c][k][inner : inner + 4]

    by_side(which, work)


class Restriction:
    def __init__(self, weights, forcing_ref, smooth_ref, shift):
        self.weights, self.forcing_ref, self.smooth_ref, self.shift = weights, forcing_ref, smooth_ref, shift
        self.held = [[None] * len(weights) for _ in range(4)]
        self.rest = [[None] * len(weights) for _ in range(4)]

    def put(self, n, own, values):
        for c in range(4):
            self.smooth_ref[c, n, own.start + self.shift : own.stop + self.shift] = values[c]
            force = self.forcing_ref[c, n, own]
            for k, weight in enumerate(self.weights):
                one, two = weight[n] * values[c], weight[n] * force
                if c < 3:
                    two = two - (weight[n] - weight[n + 1]) * values[c]
                self.held[c][k] = one if n == 0 else self.held[c][k] + one
                self.rest[c][k] = two if n == 0 else self.rest[c][k] + two


def block_weights(steps, coarse):
    start = lax.axis_index("tm") * steps
    return [[hat(start + n, k) for n in range(steps + 1)] for k in range(coarse)]


def second_sweep(g, offset, u_ref, shift, it_ref, it_own, forcing_ref, coefs, masks, kinds_ref, w_ref, x_ref, put):
    steps = forcing_ref.shape[1]
    base = offset + TILE * g
    own = slice(TILE * g, TILE * g + TILE)
    chosen = kind_masks(kinds_ref[own], w_ref.shape[1] // 64)
    for n in range(steps):
        force = [forcing_ref[c, n, own] for c in range(4)]
        before = [it_ref[c, n, it_own] for c in range(3)]
        put_operand(x_ref, n, residual(tiles_at(u_ref, n + shift), before, force, base, coefs, masks), chosen)
    product = patch_product(w_ref, x_ref, steps)
    for n in range(steps):
        change = taken(product, n)
        put(n, own, [it_ref[c, n + 1, it_own] + change[c] for c in range(4)])


def second_inner_kernel(
    a_ref, b_ref, inner_ref, forcing_ref, visc_ref, kinds_ref, w_ref, smooth_ref, sums_ref, it_ref, x_ref
):
    steps, rows = forcing_ref.shape[1], forcing_ref.shape[2]
    coarse = sums_ref.shape[3]
    masks = edge_masks()
    weights = block_weights(steps, coarse)
    it_ref[:, :, TILE : rows - TILE] = inner_ref[...]

    def work(side):
        low, high = (a_ref, b_ref) if side == 0 else (b_ref, a_ref)
        it_ref[:, :, 0:TILE] = low[...]
        it_ref[:, :, rows - TILE : rows] = high[...]

    by_side(0, work)
    for g in range(1, rows // TILE - 1):
        sums = Restriction(weights, forcing_ref, smooth_ref, -TILE)
        coefs = coefficients(visc_ref, TILE * g, masks)
        own = slice(TILE * g, TILE * g + TILE)
        second_sweep(
            g, 0, it_ref, 1, it_ref, own, forcing_ref, coefs, masks, kinds_ref, w_ref, x_ref, sums.put
        )
        for c in range(4):
            for k in range(coarse):
                sums_ref[g - 1, 0, c, k] = sums.held[c][k]
                sums_ref[g - 1, 1, c, k] = sums.rest[c][k]


def second_side_kernel(
    it_ref,
    inner_ref,
    forcing_ref,
    first_ref,
    in_ref,
    visc_loc,
    kinds_ref,
    w_ref,
    after_ref,
    smooth_ref,
    sums_ref,
    halo_ref,
    v_ref,
    x_ref,
    *,
    which,
):
    steps, rows = forcing_ref.shape[1], forcing_ref.shape[2]
    coarse = sums_ref.shape[2]
    kinds = w_ref.shape[1] // 64
    space = lax.axis_index("space")
    count = 16 * steps
    static = 16 * (steps + 1)
    masks = edge_masks()
    weights = block_weights(steps, coarse)

    def beside(side, inside, outer, edge, sign, exists):
        kappa = 0.5 * (visc_loc[inside : inside + 4] + visc_loc[outer : outer + 4])
        sums = [[None] * coarse for _ in range(4)]
        plain = [[None] * coarse for _ in range(4)]
        for n in range(steps):
            mine = [v_ref[c, n, inside : inside + 4] for c in range(4)]
            add = [kappa * mine[c] for c in range(3)]
            add[0] = add[0] - (0.5 * sign) * mine[3]
            add.append(stabilize * mine[3] + (0.5 * sign) * mine[0])
            for c in range(4):
                at = count + (c * steps + n) * 4
                rounded = (in_ref[at : at + 4] + add[c]).astype(BF16).astype(F32)
                value = v_ref[c, n, outer : outer + 4]
                for k in range(coarse):
                    one, two = weights[k][n] * rounded, weights[k][n] * value
                    sums[c][k] = one if n == 0 else sums[c][k] + one
                    plain[c][k] = two if n == 0 else plain[c][k] + two
        kind_rows = first_ref[static + 4 : static + 8]
        chosen = kind_masks(jnp.concatenate([kind_rows] * 2, axis=0), kinds)
        for k in range(coarse):
            tiles = []
            for c in range(4):
                at = 2 * count + (c * coarse + k) * 4
                far = in_ref[at : at + 4]
                pair = [far, sums[c][k]] if side == 0 else [sums[c][k], far]
                tiles.append(jnp.concatenate(pair, axis=0))
            high = [tile.astype(BF16).astype(F32) for tile in tiles]
            put_operand(x_ref, 2 * k, high, chosen)
            put_operand(x_ref, 2 * k + 1, [t - h for t, h in zip(tiles, high)], chosen)
        product = patch_product(w_ref, x_ref, 2 * coarse)
        exists = jnp.where(exists, 1.0, 0.0).astype(F32)
        for k in range(coarse):
            one, two = taken(product, 2 * k), taken(product, 2 * k + 1)
            for c in range(4):
                change = (one[c] + two[c])[edge : edge + 4]
                halo_ref[c, k] = exists * (plain[c][k] + change)

    def work(side):
        g = 0 if side == 0 else rows // TILE - 1
        if side == 0:
            inside, outer, edge, sign = 8, 4, 4, 1.0
            exists = space > 0
            v_ref[:, :, 16:20] = inner_ref[:, 1:, 0:4]
        else:
            inside, outer, edge, sign = 12, 16, 0, -1.0
            exists = space < lax.axis_size("space") - 1
            v_ref[:, :, 4:8] = inner_ref[:, 1:, rows - 2 * TILE - 4 : rows - 2 * TILE]
        v_ref[:, :, 8:16] = it_ref[:, 1:]
        for c in range(4):
            for n in range(steps):
                at = (c * steps + n) * 4
                v_ref[c, n, outer : outer + 4] = in_ref[at : at + 4]

        if which:
            beside(side, inside, outer, edge, sign, exists)
        totals = Restriction(weights, forcing_ref, smooth_ref, -TILE * g)
        coefs = coefficients(visc_loc, 8, masks)
        second_sweep(
            g, 8 - TILE * g, v_ref, 0, it_ref, slice(0, 8), forcing_ref, coefs, masks, kinds_ref, w_ref, x_ref, totals.put
        )
        for c in range(4):
            for k in range(coarse):
                sums_ref[0, c, k] = totals.held[c][k]
                sums_ref[1, c, k] = totals.rest[c][k]
                if not which:
                    halo_ref[c, k] = totals.held[c][k][4 - edge : 8 - edge]

    by_side(which, work)


def parts_kernel(
    a_sums_ref,
    b_sums_ref,
    a_halo_ref,
    b_halo_ref,
    a_visc_ref,
    b_visc_ref,
    inner_sums_ref,
    visc_ref,
    keep_ref,
    give_ref,
    s_ref,
    rest_ref,
    visc_pad,
    part_ref,
):
    size_t, _, coarse, share, _ = part_ref.shape
    rows = visc_ref.shape[0]
    groups = rows // TILE
    end = 8 + rows
    visc_pad[8:end] = visc_ref[...]
    s_ref[:, :, 16 : end - 8] = jnp.concatenate([inner_sums_ref[g, 0] for g in range(groups - 2)], axis=2)
    rest_ref[:, :, 8 : rows - 8] = jnp.concatenate([inner_sums_ref[g, 1] for g in range(groups - 2)], axis=2)

    def work(side):
        a = (a_sums_ref, a_halo_ref, a_visc_ref)
        b = (b_sums_ref, b_halo_ref, b_visc_ref)
        low, high = (a, b) if side == 0 else (b, a)
        s_ref[:, :, 8:16] = low[0][0]
        s_ref[:, :, end - 8 : end] = high[0][0]
        rest_ref[:, :, 0:8] = low[0][1]
        rest_ref[:, :, rows - 8 : rows] = high[0][1]
        s_ref[:, :, 4:8] = low[1][...]
        s_ref[:, :, end : end + 4] = high[1][...]
        visc_pad[4:8] = low[2][4:8]
        visc_pad[end : end + 4] = high[2][16:20]

    by_side(0, work)
    masks = edge_masks()
    for g in range(groups):
        base = 8 + TILE * g
        coefs = coefficients(visc_pad, base, masks)
        for k in range(coarse):
            applied = space_operator(tiles_at(s_ref, k), base, coefs, masks)
            for c in range(4):
                value = rest_ref[c, k, TILE * g : TILE * g + TILE] - applied[c]
                for row in range(0, TILE, share):
                    part_ref[(TILE * g + row) // share, c, k] = value[row : row + share]
    core = lax.axis_index("tm") % 2
    for i in range(size_t // 2):
        keep_ref[i] = part_ref[2 * i + core]
        give_ref[i] = part_ref[2 * i + (1 - core)]


def join_kernel(a_ref, b_ref, inner_ref, smooth_ref):
    rows = smooth_ref.shape[2]
    smooth_ref[:, :, TILE : rows - TILE] = inner_ref[...]

    def work(side):
        low, high = (a_ref, b_ref) if side == 0 else (b_ref, a_ref)
        smooth_ref[:, :, 0:TILE] = low[...]
        smooth_ref[:, :, rows - TILE : rows] = high[...]

    by_side(0, work)


def pair_kernel(keep_ref, given_ref, *refs, order):
    out_refs, sum_ref = refs[:-1], refs[-1]
    chip = lax.axis_index("tm") // 2
    sum_ref[...] = keep_ref[...] + given_ref[...]
    for d, ref in zip(order, out_refs):
        ref[...] = sum_ref[chip ^ d]


def total_kernel(*refs):
    out_ref = refs[-1]
    total = refs[0][...]
    for ref in refs[1:-1]:
        total = total + ref[...]
    for row in range(total.shape[2]):
        out_ref[:, :, 128 * row : 128 * row + 128] = total[:, :, row]


def whole_spec():
    return pl.BlockSpec(memory_space=pltpu.VMEM)


def call(kernel, outs, ins, scratch=(), specs=None, flops=10**6, limit=24, **options):
    size = sum(a.size * a.dtype.itemsize for a in ins)
    size += sum(o.size * o.dtype.itemsize for o in outs)
    return pl.pallas_call(
        kernel,
        out_shape=outs,
        in_specs=specs or [whole_spec()] * len(ins),
        out_specs=[whole_spec()] * len(outs),
        scratch_shapes=list(scratch),
        compiler_params=pltpu.CompilerParams(vmem_limit_bytes=int(limit * 2**20)),
        cost_estimate=pl.CostEstimate(flops=flops, bytes_accessed=size, transcendentals=0),
        **options,
    )(*ins)


def swapped(messages):
    size = lax.axis_size("space")
    out = []
    for number, message in enumerate(messages):
        pairs = [(i, i + 1) for i in range(number, size - 1, 2)]
        out.append(lax.ppermute(message, "space", pairs + [(j, i) for i, j in pairs]))
    return out


def shape_of(*dims, kind=F32):
    return jax.ShapeDtypeStruct(dims, kind)


def per_device(initial_guess, forcing, visc_table, visc_class, inverse_bank, patch_kind):
    comps, steps, planes, ny, nz = initial_guess.shape
    rows = planes * ny
    guess = initial_guess.reshape(comps, steps, rows, nz)
    force = forcing.reshape(comps, steps, rows, nz)
    kinds = inverse_bank.shape[0]
    size_t = lax.axis_size("tm")
    coarse = steps * size_t // FACTOR
    half = size_t // 2
    share = rows // size_t

    (tail,) = call(
        tail_kernel,
        [shape_of(comps, 2, rows, nz)],
        [guess, force],
        specs=[
            pl.BlockSpec((comps, 2, rows, nz), lambda i: (0, steps // 2 - 1, 0, 0)),
            pl.BlockSpec((comps, 1, rows, nz), lambda i: (0, steps - 1, 0, 0)),
        ],
        limit=53.5,
        grid=(1,),
    )
    tail = lax.ppermute(tail, "tm", [(i, i + 1) for i in range(size_t - 1)])

    visc, kind_rows, weights = call(
        tables_kernel,
        [shape_of(rows, nz), shape_of(rows, nz), shape_of(64, 64 * kinds, kind=BF16)],
        [visc_table, visc_class, inverse_bank, patch_kind],
        [pltpu.VMEM((rows // 4, nz // 2), F32)],
        [pl.BlockSpec(memory_space=pltpu.SMEM)] + [whole_spec()] * 3,
    )

    last = rows // 8 - 1
    edge = (comps, steps, 8, nz)
    t_edge = (comps, 1, 8, nz)
    length = comps * (steps + 1) * 4 + 8
    first = call(
        first_message_kernel,
        [shape_of(length, nz)] * 2,
        [guess, guess, tail, tail, visc, kind_rows],
        specs=[
            pl.BlockSpec(edge, lambda i: (0, 0, 0, 0)),
            pl.BlockSpec(edge, lambda i: (0, 0, last, 0)),
            pl.BlockSpec(t_edge, lambda i: (0, 0, 0, 0)),
            pl.BlockSpec(t_edge, lambda i: (0, 0, last, 0)),
            whole_spec(),
            whole_spec(),
        ],
        grid=(1,),
    )
    first_in = swapped(first)

    field = shape_of(comps, steps, rows, nz)
    operand = pltpu.VMEM((64 * kinds, (steps + 1) * nz), BF16)
    (inner,) = call(
        first_inner_kernel,
        [shape_of(comps, steps + 1, rows - 2 * TILE, nz)],
        [guess, force, tail, visc, kind_rows, weights],
        [operand],
        flops=10**7,
    )
    length_2 = 8 * comps * steps + 4 * comps * coarse
    done = []
    messages = [shape_of(4 * comps * steps, nz), shape_of(length_2, nz)]
    for which in range(2):
        done.append(
            call(
                functools.partial(first_side_kernel, which=which, coarse=coarse),
                [shape_of(comps, steps + 1, TILE, nz), messages[which], shape_of(24, nz)],
                [guess, force, tail, inner, first_in[which], visc, kind_rows, weights]
                + [made[2] for made in done],
                [pltpu.VMEM((comps, steps + 1, 24, nz), F32)]
                + [pltpu.VMEM((comps, steps, 24, nz), F32)] * which
                + [operand],
                flops=5 * 10**6,
            )
        )
    iterate, second, visc_loc = zip(*done)
    second_in = swapped(second)

    inner_smooth, inner_sums = call(
        second_inner_kernel,
        [shape_of(comps, steps, rows - 2 * TILE, nz), shape_of(rows // TILE - 2, 2, comps, coarse, TILE, nz)],
        [*iterate, inner, force, visc, kind_rows, weights],
        [pltpu.VMEM((comps, steps + 1, rows, nz), F32), operand],
        flops=10**10,
    )
    done = []
    for which in range(2):
        done.append(
            call(
                functools.partial(second_side_kernel, which=which),
                [
                    shape_of(comps, steps, TILE, nz),
                    shape_of(2, comps, coarse, TILE, nz),
                    shape_of(comps, coarse, 4, nz),
                ],
                [iterate[which], inner, force, first_in[which], second_in[which]]
                + [visc_loc[which], kind_rows, weights, done[0][2] if which else visc],
                [
                    pltpu.VMEM((comps, steps, 24, nz), F32),
                    pltpu.VMEM((64 * kinds, max(steps, 2 * coarse) * nz), BF16),
                ],
                flops=5 * 10**6,
            )
        )
    smooth, sums, (face, halo) = zip(*done)
    (face,) = swapped([face])
    piece = (comps, coarse, share, nz)
    keep, give = call(
        parts_kernel,
        [shape_of(half, *piece)] * 2,
        [*sums, face, halo, *visc_loc, inner_sums, visc],
        [
            pltpu.VMEM((comps, coarse, rows + 16, nz), F32),
            pltpu.VMEM((comps, coarse, rows, nz), F32),
            pltpu.VMEM((rows + 16, nz), F32),
            pltpu.VMEM((size_t, *piece), F32),
        ],
    )
    given = lax.ppermute(give, "tm", [(i, i ^ 1) for i in range(size_t)])
    (smoothed,) = call(join_kernel, [field], [*smooth, inner_smooth])
    far_first = list(range(half - 1, 0, -1))
    far_first[:2] = far_first[1::-1]
    *others, own = call(
        functools.partial(pair_kernel, order=far_first + [0]),
        [shape_of(*piece)] * half,
        [keep, given],
        [pltpu.VMEM((half, *piece), F32)],
    )
    arrived = [
        lax.ppermute(other, "tm", [(i, i ^ (2 * d)) for i in range(size_t)])
        for d, other in zip(far_first, others)
    ]
    (result,) = call(total_kernel, [shape_of(comps, coarse, share * nz)], [*arrived, own])
    return (smoothed.reshape(initial_guess.shape), result)


def solution(mesh):
    return jax.shard_map(
        per_device,
        mesh=mesh,
        in_specs=(
            P(None, "tm", "space", None, None),
            P(None, "tm", "space", None, None),
            P(),
            P("space", None, None),
            P(),
            P("space", None, None),
        ),
        out_specs=(P(None, "tm", "space", None, None), P(None, None, ("space", "tm"))),
        check_vma=False,
    )
```
